128 devices in a mesh: row: 4 (over x), col: 2 (over z_hi), ga: 16 (over z_lo, y, core).
Axes of the slice: x: 4, y: 4, z: 4 (z_hi: 2, z_lo: 2; z = z_hi * 2 + z_lo), core: 2. Of those that a mesh axis runs over, the one named last changes fastest.
Arguments:
- matrix_elements: bfloat16 [2, 2, 2048, 2048], P(None, None, 'ga', ('row', 'col')), may hold values from -6 to 6
- screening: bfloat16 [2, 2, 2048, 2048], P(None, None, 'ga'), may hold values from -0.09375 to 0.09375
- pair_list: int32 [3, 2], replicated, may hold values from 0 to 1, as said below
- pair_q: int32 [3], replicated, may hold values from 0 to 1, as said below
Outputs:
- direct_kernel: bfloat16 [3, 2048, 2, 2048], P(None, 'ga', None, ('row', 'col'))
The draws below stay inside these ranges and needn't reach their ends.
Inputs may be any that keep to these rules, and one draw needn't show every extreme that they name: `pair_list`: each row is a pair (k, k') with k <= k'; no pair appears twice; every difference k' - k from 0 to 1 occurs. `pair_q`: rows with equal k' - k have equal entries and rows with different k' - k different ones.
All inputs are finite; a program needn't handle non-finite values.
Results may differ from the reference program's by a relative error of at most 0.022.
Values may be sent and summed in bfloat16 or wider, within the bound.
No kernel may reach another device: no remote copies, remote signals or barrier semaphores. Data moves between devices by JAX's collectives and lax.ppermute only.
A program may use at most 64 MiB of HBM per device.

```python
import math
import jax
import jax.numpy as jnp
import numpy as np
from jax import lax

NK = 2
G = 2048
T_SIZE = 2048
NQ = 2
NPAIR = 3
N_GA = 16


def pair_draws(key):
    listing = [[leading, trailing] for leading in range(NK) for trailing in range(leading, NK)]
    pair_table = np.array(listing, dtype=np.int32)
    count_all = pair_table.shape[0]
    index_grid = np.zeros((NK, NK), dtype=np.int32)
    for position in range(count_all):
        index_grid[listing[position][0], listing[position][1] - listing[position][0]] = position
    offsets = jnp.arange(NK, dtype=jnp.int32)
    start_counts = NK - offsets
    random_draw = jax.random.randint(jax.random.fold_in(key, 11), (NK,), 0, 1 << 20).astype(jnp.int32)
    starts = jnp.where(offsets == 0, 1 + random_draw % (NK - 1), random_draw % start_counts)
    forced = jnp.asarray(index_grid)[starts, offsets]
    scores = jax.random.permutation(jax.random.fold_in(key, 12), count_all).astype(jnp.int32)
    scores = scores.at[forced].set(offsets - count_all)
    chosen = jnp.argsort(scores, stable=True)[:NPAIR]
    ordering = jax.random.permutation(jax.random.fold_in(key, 13), NPAIR)
    pair_rows = jnp.asarray(pair_table)[chosen[ordering]]
    q_lookup = jax.random.permutation(jax.random.fold_in(key, 14), NQ).astype(jnp.int32)
    return (pair_rows, q_lookup[pair_rows[:, 1] - pair_rows[:, 0]])


def draw_pair_list(key, part):
    return pair_draws(key)[0]


def draw_pair_q(key, part):
    return pair_draws(key)[1]


def spiked(entries, key, source, target, parts, factor):
    def block_of(dim):
        return (jnp.arange(entries.shape[dim]) // (entries.shape[dim] // parts)).reshape((-1,) + (1,) * (entries.ndim - 1 - dim))

    one_side = jax.random.permutation(key, parts)[block_of(target)]
    other_side = (block_of(target) + parts // 2) % parts
    return jnp.where((block_of(source) == one_side) | (block_of(source) == other_side), factor * entries, entries)


def block_scale(key, extent, shards, smallest, high):
    def one(dim, parts):
        heights = jax.random.uniform(jax.random.fold_in(jax.random.fold_in(key, 6), dim), (parts,), jnp.float32, smallest / len(shards), high / len(shards))
        return jnp.repeat(jnp.exp(heights), extent[dim] // parts).reshape((-1,) + (1,) * (len(extent) - dim - 1))

    loudness = one(*shards[0])
    for cut in shards[1:]:
        loudness = loudness * one(*cut)
    return loudness


def normal_values(key, shape, spread, reach, cuts=(), held_as=jnp.bfloat16):
    drawn = spread * jax.random.normal(key, shape, jnp.float32)
    if cuts:
        drawn = drawn * block_scale(key, shape, cuts, -0.22, 0.18)
    return jnp.clip(drawn, -reach, reach).astype(held_as)


def bell_draw_with(own_key, shape, scale, reach, shards, heavy, kind=jnp.bfloat16):
    result = scale * jax.random.normal(own_key, shape, jnp.float32)
    if shards:
        result = result * block_scale(own_key, shape, shards, -0.22, 0.18)
    return jnp.clip(spiked(result, jax.random.fold_in(own_key, 3), *heavy), -reach, reach).astype(kind)


def setup_inputs(seed: int = 0) -> dict:
    arg_keys = jax.random.split(jax.random.key(seed), 5)
    matrix_elements = bell_draw_with(arg_keys[0], (NK, 2, G, T_SIZE), 1.0, 6.0, ((2, 16), (3, 8)), (2, 3, 16, 2.0))
    screening = normal_values(arg_keys[1], (NQ, 2, G, G), (2 * G) ** -0.5, 0.09375, ((2, 16),))
    pair_list = draw_pair_list(jax.random.fold_in(arg_keys[4], 71), 0)
    pair_q = draw_pair_q(jax.random.fold_in(arg_keys[4], 71), 0)
    return {"matrix_elements": matrix_elements, "screening": screening, "pair_list": pair_list, "pair_q": pair_q}


def apply_screening(weights, columns):
    real_part = jnp.dot(weights[0], columns[0], preferred_element_type=jnp.float32) - jnp.dot(weights[1], columns[1], preferred_element_type=jnp.float32)
    imag_part = jnp.dot(weights[0], columns[1], preferred_element_type=jnp.float32) + jnp.dot(weights[1], columns[0], preferred_element_type=jnp.float32)
    return (real_part, imag_part)

def reference(matrix_elements, screening, pair_list, pair_q):
    factor = 1.0 / math.sqrt(2.0 * G)
    block_rows = G // N_GA
    kernels = []
    for position in range(NPAIR):
        left_rows = matrix_elements[pair_list[position, 0]]
        right_rows = matrix_elements[pair_list[position, 1]]
        weights = screening[pair_q[position]]
        real_part, imag_part = apply_screening(weights, right_rows)
        screened = jnp.stack((real_part, imag_part), 0).astype(jnp.bfloat16)
        left_blocks = left_rows.reshape(2, N_GA, block_rows, T_SIZE).transpose(1, 0, 2, 3)
        screen_blocks = screened.reshape(2, N_GA, block_rows, T_SIZE).transpose(1, 0, 2, 3)

        def add_block(running, pieces):
            left_part, screen_part = pieces
            part_re = jnp.dot(left_part[0].T, screen_part[0], preferred_element_type=jnp.float32) + jnp.dot(left_part[1].T, screen_part[1], preferred_element_type=jnp.float32)
            part_im = jnp.dot(left_part[0].T, screen_part[1], preferred_element_type=jnp.float32) - jnp.dot(left_part[1].T, screen_part[0], preferred_element_type=jnp.float32)
            rounded = lax.optimization_barrier((jnp.stack((part_re, part_im), 1) * factor).astype(jnp.bfloat16))
            return (running + rounded.astype(jnp.float32), None)
        running, unused = lax.scan(add_block, jnp.zeros((T_SIZE, 2, T_SIZE), jnp.float32), (left_blocks, screen_blocks))
        kernels.append(running.astype(jnp.bfloat16))
    return jnp.stack(kernels, 0)
```

```python
import functools
import math

import jax
import jax.numpy as jnp
from jax import lax
from jax.experimental import pallas as pl
from jax.experimental.pallas import tpu as pltpu
from jax.sharding import Mesh, PartitionSpec as P

BF = jnp.bfloat16
F32 = jnp.float32
VMEM = pl.BlockSpec(memory_space=pltpu.VMEM)
SMEM = pl.BlockSpec(memory_space=pltpu.SMEM)
LIMIT = 24 * 1024 * 1024
PAIRS = ((0, 0), (0, 1), (1, 1))


def call(body, outs, *args, scratch=(), smem=0):
    return pl.pallas_call(
        body,
        out_shape=[jax.ShapeDtypeStruct(s, BF) for s in outs],
        in_specs=[SMEM] * smem + [VMEM] * (len(args) - smem),
        out_specs=[VMEM] * len(outs),
        scratch_shapes=list(scratch),
        compiler_params=pltpu.CompilerParams(vmem_limit_bytes=LIMIT),
    )(*args)


def shift(x, axis, size, step):
    return lax.ppermute(x, axis, [(i, (i + step) % size) for i in range(size)])


def transpose_halves(m_ref, mine_ref, other_ref):
    c = lax.axis_index("c")
    for k in range(2):
        for part in range(2):
            lanes = slice(part * 128, (part + 1) * 128)
            mine_ref[k, :, lanes] = m_ref[k, part, :, pl.ds(pl.multiple_of(c * 128, 128), 128)].T
            other_ref[k, :, lanes] = m_ref[k, part, :, pl.ds(pl.multiple_of((1 - c) * 128, 128), 128)].T


def join_halves(mine_ref, got_ref, out_ref):
    out_ref[:, :, :256] = mine_ref[...]
    out_ref[:, :, 256:] = got_ref[...]


def weight_rows(list_ref, q_ref, own_ref, mate_ref, out_ref):
    zl, y, c = lax.axis_index("zl"), lax.axis_index("y"), lax.axis_index("c")
    for slot, (k, kp) in enumerate(((0, 0), (0, 1))):
        q = q_ref[0]
        for r in range(1, 3):
            hit = (list_ref[r, 0] == k) & (list_ref[r, 1] == kp)
            q = jnp.where(hit, q_ref[r], q)
        for b in range(2):
            for s in range(4):
                block = (zl ^ b) * 4 + lax.rem(y + s, 4)
                lanes = pl.ds(pl.multiple_of(block * 256 + c * 128, 128), 128)
                col = (b * 4 + s) * 256
                for o, ref in enumerate((own_ref, mate_ref)):
                    re, im = ref[q, 0, :, lanes], ref[q, 1, :, lanes]
                    row = o * 256
                    out_ref[slot, row : row + 128, col : col + 128] = re
                    out_ref[slot, row : row + 128, col + 128 : col + 256] = -im
                    out_ref[slot, row + 128 : row + 256, col : col + 128] = im
                    out_ref[slot, row + 128 : row + 256, col + 128 : col + 256] = re


def screen(w_ref, *refs):
    shards, out_ref, acc = refs[:8], refs[8], refs[9]
    for i, ref in enumerate(shards):
        cols = slice(i * 256, (i + 1) * 256)
        for p, (k, kp) in enumerate(PAIRS):
            term = jnp.dot(
                w_ref[kp - k, :, cols], ref[kp].reshape(256, 256), preferred_element_type=F32
            )
            if i == 0:
                acc[p] = term
            else:
                acc[p] += term
    out_ref[...] = acc[...].reshape(3, 2, 2, 128, 256).astype(BF)


def sort_rows(*refs):
    shards, out_ref = refs[:8], refs[8]
    x, zh, zl, y = (lax.axis_index(a) for a in ("x", "zh", "zl", "y"))
    for dz in range(2):
        for dx in range(4):
            j = lax.rem(x + dx, 4) * 2 + (zh ^ dz)
            b, s = (j // 4) ^ zl, lax.rem((j % 4) - y + 4, 4)
            out_ref[:, b * 4 + s] = shards[dz * 4 + dx][...]


def contract(factor, mine_ref, got_ref, rows_ref, ak_ref, as_ref, bk_ref, b1_ref, b2_ref, b3_ref):
    for p, (k, kp) in enumerate(PAIRS):
        blocks = []
        for o in range(2):
            re = (mine_ref[p, o, 0].astype(F32) + got_ref[p, 1 - o, 0].astype(F32)).astype(BF)
            im = (mine_ref[p, o, 1].astype(F32) + got_ref[p, 1 - o, 1].astype(F32)).astype(BF)
            blocks += [jnp.concatenate((re, im), 1), jnp.concatenate((im, -re), 1)]
        rhs = jnp.concatenate(blocks, 0)
        for b in range(2):
            for s in range(4):
                part = jnp.dot(rows_ref[k, b * 4 + s], rhs, preferred_element_type=F32)
                part = (part * factor).astype(BF)
                a_part = part if p == 0 else part[:, :256] if p == 2 else None
                b_part = part if p == 1 else part[:, 256:] if p == 2 else None
                if a_part is not None:
                    lanes = slice(0, 512) if p == 0 else slice(512, 768)
                    (ak_ref, as_ref)[b][s, :, lanes] = a_part
                if b_part is not None:
                    lanes = slice(0, 512) if p == 1 else slice(512, 768)
                    (bk_ref, b1_ref, b2_ref, b3_ref)[s][b, :, lanes] = b_part


def add_a(keep_ref, got_ref, *outs):
    for s, ref in enumerate(outs):
        ref[...] = (keep_ref[s].astype(F32) + got_ref[s].astype(F32)).astype(BF)


def add_b(keep_ref, g1_ref, g2_ref, g3_ref, out_ref, send_ref):
    total = [keep_ref[b].astype(F32) + g1_ref[b].astype(F32) + (g2_ref[b].astype(F32) + g3_ref[b].astype(F32)) for b in range(2)]
    out_ref[...] = total[0].astype(BF)
    send_ref[...] = total[1].astype(BF)


def finish(list_ref, a0_ref, a1_ref, a2_ref, a3_ref, b0_ref, b1_ref, out_ref):
    a = a0_ref[...].astype(F32) + a1_ref[...].astype(F32) + (a2_ref[...].astype(F32) + a3_ref[...].astype(F32))
    b = b0_ref[...].astype(F32) + b1_ref[...].astype(F32)
    sums = (a[:, :512], b[:, :512], jnp.concatenate((a[:, 512:], b[:, 512:]), 1))
    for (k, kp), value in zip(PAIRS, sums):
        place = 0
        for r in range(1, 3):
            place = jnp.where((list_ref[r, 0] == k) & (list_ref[r, 1] == kp), r, place)
        out_ref[place] = value.astype(BF)


def gather(x, swap_axis, ring_axis):
    mate = shift(x, swap_axis, 2, 1)
    own = [x, shift(x, ring_axis, 4, -1), shift(x, ring_axis, 4, 2), shift(x, ring_axis, 4, 1)]
    far = [mate, shift(mate, ring_axis, 4, -1), shift(own[2], swap_axis, 2, 1), shift(mate, ring_axis, 4, 1)]
    return own + far


def per_device(matrix_elements, screening, pair_list, pair_q):
    factor = 1.0 / math.sqrt(2.0 * screening.shape[3])
    columns = gather(matrix_elements, "zl", "y")
    mate_weights = shift(screening, "c", 2, 1)
    mine, other = call(transpose_halves, [(2, 128, 256)] * 2, matrix_elements)
    (rows,) = call(join_halves, [(2, 128, 512)], mine, shift(other, "c", 2, 1))
    row_shards = gather(rows, "zh", "x")
    (weights,) = call(weight_rows, [(2, 512, 2048)], pair_list, pair_q, screening, mate_weights, smem=2)
    (part,) = call(screen, [(3, 2, 2, 128, 256)], weights, *columns, scratch=[pltpu.VMEM((3, 512, 256), F32)])
    (sorted_rows,) = call(sort_rows, [(2, 8, 128, 512)], *row_shards)
    got = shift(part, "c", 2, 1)
    ak, asend, bk, b1, b2, b3 = call(
        functools.partial(contract, factor), [(4, 128, 768)] * 2 + [(2, 128, 768)] * 4, part, got, sorted_rows
    )
    a_got = shift(asend, "zl", 2, 1)
    b_got = [shift(b1, "y", 4, 1), shift(b2, "y", 4, 2), shift(b3, "y", 4, -1)]
    q = call(add_a, [(128, 768)] * 4, ak, a_got)
    b_keep, b_send = call(add_b, [(128, 768)] * 2, bk, *b_got)
    a_last = [shift(q[1], "y", 4, 1), shift(q[2], "y", 4, 2), shift(q[3], "y", 4, -1)]
    b_last = shift(b_send, "zl", 2, 1)
    (out,) = call(finish, [(3, 128, 512)], pair_list, q[0], *a_last, b_keep, b_last, smem=1)
    return out.reshape(3, 128, 2, 256)


def solution(mesh):
    split = Mesh(mesh.devices.reshape(4, 2, 2, 4, 2), ("x", "zh", "zl", "y", "c"))
    ga = ("zl", "y", "c")
    return jax.shard_map(
        per_device,
        mesh=split,
        in_specs=(P(None, None, ga, ("x", "zh")), P(None, None, ga, None), P(), P()),
        out_specs=P(None, ga, None, ("x", "zh")),
        check_vma=False,
    )
```

```python
import functools
import math

import jax
import jax.numpy as jnp
from jax import lax
from jax.experimental import pallas as pl
from jax.experimental.pallas import tpu as pltpu
from jax.sharding import Mesh, PartitionSpec as P

BF = jnp.bfloat16
F32 = jnp.float32
MIB = 1024 * 1024
VMEM = pl.BlockSpec(memory_space=pltpu.VMEM)
SMEM = pl.BlockSpec(memory_space=pltpu.SMEM)
ANY = pl.BlockSpec(memory_space=pl.ANY)
PAIRS = ((0, 0), (0, 1), (1, 1))
CUT = 256
WIDE_Y = 512 + CUT
WIDE_Z = 1024 - CUT


def call(body, outs, specs, *args, scratch=(), limit=2):
    return pl.pallas_call(
        body,
        out_shape=[jax.ShapeDtypeStruct(s, BF) for s in outs],
        in_specs=specs,
        out_specs=[VMEM] * len(outs),
        scratch_shapes=list(scratch),
        compiler_params=pltpu.CompilerParams(vmem_limit_bytes=limit * MIB),
    )(*args)


def copy_all(moves, sems):
    copies = [pltpu.make_async_copy(src, dst, sems.at[i]) for i, (src, dst) in enumerate(moves)]
    for copy in copies:
        copy.start()
    return copies


def transpose_halves(m_ref, mine_ref, other_ref):
    c = lax.axis_index("c")
    for k in range(2):
        for part in range(2):
            lanes = slice(part * 128, (part + 1) * 128)
            mine_ref[k, :, lanes] = m_ref[k, part, :, pl.ds(pl.multiple_of(c * 128, 128), 128)].T
            other_ref[k, :, lanes] = m_ref[k, part, :, pl.ds(pl.multiple_of((1 - c) * 128, 128), 128)].T


def join_halves(mine_ref, got_ref, out_ref):
    out_ref[:, :, :256] = mine_ref[...]
    out_ref[:, :, 256:] = got_ref[...]


def join(a_ref, b_ref, out_ref, sems):
    for copy in copy_all([(a_ref, out_ref.at[0]), (b_ref, out_ref.at[1])], sems):
        copy.wait()


def ring_masks():
    c = lax.axis_index("c")
    return (0, 1 + 2 * c, 3 - 2 * c, 2)


def pair_row(list_ref, pair):
    row = 0
    for r in range(1, 3):
        row = jnp.where((list_ref[0, r] == pair[0]) & (list_ref[1, r] == pair[1]), r, row)
    return row


def weight_rows(list_ref, q_ref, own_ref, mate_ref, out_ref, held, sems):
    zl, y, c = lax.axis_index("zl"), lax.axis_index("y"), lax.axis_index("c")
    moves = []
    for slot in range(2):
        q = q_ref[pair_row(list_ref, PAIRS[slot])]
        for o, ref in enumerate((own_ref, mate_ref)):
            moves.append((ref.at[q], held.at[slot, o]))
    copies = copy_all(moves, sems)
    for slot in range(2):
        for o in range(2):
            copies[slot * 2 + o].wait()
            for b in range(2):
                for s, mask in enumerate(ring_masks()):
                    block = (zl ^ b) * 4 + (y ^ mask)
                    lanes = pl.ds(pl.multiple_of(block * 256 + c * 128, 128), 128)
                    re, im = held[slot, o, 0, :, lanes], held[slot, o, 1, :, lanes]
                    row, col = o * 256, (b * 4 + s) * 256
                    out_ref[slot, row : row + 128, col : col + 128] = re
                    out_ref[slot, row : row + 128, col + 128 : col + 256] = -im
                    out_ref[slot, row + 128 : row + 256, col : col + 128] = im
                    out_ref[slot, row + 128 : row + 256, col + 128 : col + 256] = re


def screen(w_ref, *refs):
    pieces, (out_ref, acc, held, sems) = refs[:4], refs[4:]
    copies = copy_all([(ref, held.at[i]) for i, ref in enumerate(pieces)], sems)
    for i in range(8):
        if i % 2 == 0:
            copies[i // 2].wait()
        cols = slice(i * 256, (i + 1) * 256)
        for p, (k, kp) in enumerate(PAIRS):
            rhs = held[i // 2, i % 2, kp].reshape(256, 256)
            term = jnp.dot(w_ref[kp - k, :, cols], rhs, preferred_element_type=F32)
            if i == 0:
                acc[p] = term
            else:
                acc[p] += term
    out_ref[...] = acc[...].reshape(3, 2, 2, 128, 256).astype(BF)


def right_side(p, mine_ref, got_ref):
    blocks = []
    for o in range(2):
        re = (mine_ref[p, o, 0].astype(F32) + got_ref[p, 1 - o, 0].astype(F32)).astype(BF)
        im = (mine_ref[p, o, 1].astype(F32) + got_ref[p, 1 - o, 1].astype(F32)).astype(BF)
        blocks += [jnp.concatenate((re, im), 1), jnp.concatenate((im, -re), 1)]
    return jnp.concatenate(blocks, 0)


def rows_for(b, s, k, pieces):
    x, zh, zl, y, c = (lax.axis_index(a) for a in ("x", "zh", "zl", "y", "c"))
    j = (zl ^ b) * 4 + lax.rem(y + s, 4)
    mask = (j // 2) ^ x
    near = (mask == 0) | (mask == 1 + 2 * c)
    unit = jnp.where((mask == 0) | (mask == 3 - 2 * c), 0, 1)
    same = lax.rem(j, 2) == zh
    values = [ref[unit, k] for ref in pieces]
    own = jnp.where(near, values[0], values[1])
    far = jnp.where(near, values[2], values[3])
    return jnp.where(same, own, far)


def contract_y(factor, mine_ref, got_ref, r0, r1, r2, r3, k_ref, s1_ref, s2_ref, s3_ref, rest_ref):
    rhs = [right_side(p, mine_ref, got_ref) for p in range(2)]
    for b in range(2):
        for s, ref in enumerate((k_ref, s1_ref, s2_ref, s3_ref)):
            rows = rows_for(b, s, 0, (r0, r1, r2, r3))
            for p in range(2):
                part = jnp.dot(rows, rhs[p], preferred_element_type=F32)
                part = (part * factor).astype(BF)
                if p == 0:
                    ref[b, :, :512] = part
                else:
                    ref[b, :, 512:] = part[:, :CUT]
                    rest_ref[b, s] = part[:, CUT:]


def contract_z(factor, mine_ref, got_ref, r0, r1, r2, r3, rest_ref, k_ref, s_ref):
    rhs = right_side(2, mine_ref, got_ref)
    for b, ref in enumerate((k_ref, s_ref)):
        for s in range(4):
            part = jnp.dot(rows_for(b, s, 1, (r0, r1, r2, r3)), rhs, preferred_element_type=F32)
            ref[s, :, :512] = (part * factor).astype(BF)
            ref[s, :, 512:] = rest_ref[b, s]


def add_z(keep_ref, got_ref, *outs):
    for s, ref in enumerate(outs):
        ref[...] = (keep_ref[s].astype(F32) + got_ref[s].astype(F32)).astype(BF)


def add_y(keep_ref, g1_ref, g2_ref, g3_ref, out_ref, send_ref):
    for b, ref in enumerate((out_ref, send_ref)):
        near = keep_ref[b].astype(F32) + g1_ref[b].astype(F32)
        ref[...] = (near + (g2_ref[b].astype(F32) + g3_ref[b].astype(F32))).astype(BF)


def finish(list_ref, z0_ref, z1_ref, z2_ref, z3_ref, y0_ref, y1_ref, out_ref):
    z = z0_ref[...].astype(F32) + z1_ref[...].astype(F32) + (z2_ref[...].astype(F32) + z3_ref[...].astype(F32))
    y = y0_ref[...].astype(F32) + y1_ref[...].astype(F32)
    sums = (y[:, :512], jnp.concatenate((y[:, 512:], z[:, 512:]), 1), z[:, :512])
    for pair, value in zip(PAIRS, sums):
        out_ref[pair_row(list_ref, pair)] = value.astype(BF)


def shift(x, axis, size, step):
    return lax.ppermute(x, axis, [(i, (i + step) % size) for i in range(size)])


def ring_swap(x, axis, second):
    pairs = [(i * 2 + c, (i ^ (3 if c ^ second else 1)) * 2 + c) for i in range(4) for c in range(2)]
    return lax.ppermute(x, (axis, "c"), pairs)


def double(x, got):
    return call(join, [(2,) + x.shape], [ANY] * 2, x, got, scratch=[pltpu.SemaphoreType.DMA((2,))])[0]


def tie(*xs):
    return lax.optimization_barrier(xs)


def per_device(matrix_elements, screening, pair_list, pair_q):
    factor = 1.0 / math.sqrt(2.0 * screening.shape[3])
    m, pairs = matrix_elements, pair_list.T
    mine, other = call(transpose_halves, [(2, 128, 256)] * 2, [VMEM], m)
    (rows,) = call(join_halves, [(2, 128, 512)], [VMEM] * 2, mine, shift(other, "c", 2, 1))
    mate_weights = shift(screening, "c", 2, 1)
    m_far = shift(m, "zl", 2, 1)
    m_got = ring_swap(m, "y", 0)
    rows_far = shift(rows, "zh", 2, 1)
    rows_got = ring_swap(rows, "x", 0)
    m_near = double(m, m_got)
    m_next = ring_swap(m_near, "y", 1)
    rows_near = double(rows, rows_got)
    rows_next = ring_swap(rows_near, "x", 1)
    m_far_got = ring_swap(m_far, "y", 0)
    m_far_got, rows_far = tie(m_far_got, rows_far)
    rows_far_got = ring_swap(rows_far, "x", 0)
    m_far_near = double(m_far, m_far_got)
    m_far_next = ring_swap(m_far_near, "y", 1)
    rows_far_near = double(rows_far, rows_far_got)
    rows_far_next = ring_swap(rows_far_near, "x", 1)
    (weights,) = call(
        weight_rows,
        [(2, 512, 2048)],
        [SMEM] * 2 + [ANY] * 2,
        pairs,
        pair_q,
        screening,
        mate_weights,
        limit=8,
        scratch=[pltpu.VMEM((2, 2, 2, 128, 2048), BF), pltpu.SemaphoreType.DMA((4,))],
    )
    weights, rows_next = tie(weights, rows_next)
    (part,) = call(
        screen,
        [(3, 2, 2, 128, 256)],
        [VMEM] + [ANY] * 4,
        weights,
        m_near,
        m_next,
        m_far_near,
        m_far_next,
        limit=8,
        scratch=[pltpu.VMEM((3, 512, 256), F32), pltpu.VMEM((4, 2, 2, 2, 128, 256), BF), pltpu.SemaphoreType.DMA((4,))],
    )
    left = [part, shift(part, "c", 2, 1), rows_near, rows_next, rows_far_near, rows_far_next]
    y_keep, y1, y2, y3, rest = call(
        functools.partial(contract_y, factor),
        [(2, 128, WIDE_Y)] * 4 + [(2, 4, 128, 512 - CUT)],
        [VMEM] * 6,
        *left,
        limit=8,
    )
    z_keep, z_send = call(
        functools.partial(contract_z, factor), [(4, 128, WIDE_Z)] * 2, [VMEM] * 7, *left, rest, limit=8
    )
    z_got = shift(z_send, "zl", 2, 1)
    y_got = [shift(y1, "y", 4, 1), shift(y2, "y", 4, 2), shift(y3, "y", 4, -1)]
    z_sums = call(add_z, [(128, WIDE_Z)] * 4, [VMEM] * 2, z_keep, z_got)
    y_keep, y_send = call(add_y, [(128, WIDE_Y)] * 2, [VMEM] * 4, y_keep, *y_got)
    z_last = [shift(z_sums[1], "y", 4, 1), shift(z_sums[2], "y", 4, 2), shift(z_sums[3], "y", 4, -1)]
    y_last = shift(y_send, "zl", 2, 1)
    (out,) = call(finish, [(3, 128, 512)], [SMEM] + [VMEM] * 6, pairs, z_sums[0], *z_last, y_keep, y_last)
    return out.reshape(3, 128, 2, 256)


def solution(mesh):
    split = Mesh(mesh.devices.reshape(4, 2, 2, 4, 2), ("x", "zh", "zl", "y", "c"))
    ga = ("zl", "y", "c")
    return jax.shard_map(
        per_device,
        mesh=split,
        in_specs=(P(None, None, ga, ("x", "zh")), P(None, None, ga, None), P(), P()),
        out_specs=P(None, ga, None, ("x", "zh")),
        check_vma=False,
    )
```

```python
import functools
import math

import jax
import jax.numpy as jnp
from jax import lax
from jax.experimental import pallas as pl
from jax.experimental.pallas import tpu as pltpu
from jax.sharding import Mesh, PartitionSpec as P

BF = jnp.bfloat16
F32 = jnp.float32
MIB = 1024 * 1024
VMEM = pl.BlockSpec(memory_space=pltpu.VMEM)
SMEM = pl.BlockSpec(memory_space=pltpu.SMEM)
ANY = pl.BlockSpec(memory_space=pl.ANY)
PAIRS = ((0, 0), (0, 1), (1, 1))
CUT = 256
WIDE_Y = 512 + CUT
WIDE_Z = 1024 - CUT


def call(body, outs, specs, *args, scratch=(), limit=2):
    return pl.pallas_call(
        body,
        out_shape=[jax.ShapeDtypeStruct(s, BF) for s in outs],
        in_specs=specs,
        out_specs=[VMEM] * len(outs),
        scratch_shapes=list(scratch),
        compiler_params=pltpu.CompilerParams(vmem_limit_bytes=limit * MIB),
    )(*args)


def copy_all(moves, sems):
    copies = [pltpu.make_async_copy(src, dst, sems.at[i]) for i, (src, dst) in enumerate(moves)]
    for copy in copies:
        copy.start()
    return copies


def transpose_halves(m_ref, mine_ref, other_ref):
    c = lax.axis_index("c")
    for k in range(2):
        for part in range(2):
            lanes = slice(part * 128, (part + 1) * 128)
            mine_ref[k, :, lanes] = m_ref[k, part, :, pl.ds(pl.multiple_of(c * 128, 128), 128)].T
            other_ref[k, :, lanes] = m_ref[k, part, :, pl.ds(pl.multiple_of((1 - c) * 128, 128), 128)].T


def join_halves(mine_ref, got_ref, out_ref):
    out_ref[:, :, :256] = mine_ref[...]
    out_ref[:, :, 256:] = got_ref[...]


def join(a_ref, b_ref, out_ref, sems):
    for copy in copy_all([(a_ref, out_ref.at[0]), (b_ref, out_ref.at[1])], sems):
        copy.wait()


def ring_masks(flip=0):
    c = lax.axis_index("c")
    c = 1 - c if flip else c
    return (0, 1 + 2 * c, 3 - 2 * c, 2)


def pair_row(list_ref, pair):
    row = 0
    for r in range(1, 3):
        row = jnp.where((list_ref[0, r] == pair[0]) & (list_ref[1, r] == pair[1]), r, row)
    return row


def weight_rows(list_ref, q_ref, own_ref, mate_ref, out_ref, held, sems):
    zl, y, c = lax.axis_index("zl"), lax.axis_index("y"), lax.axis_index("c")
    moves = []
    for slot in range(2):
        q = q_ref[pair_row(list_ref, PAIRS[slot])]
        for o, ref in enumerate((own_ref, mate_ref)):
            moves.append((ref.at[q], held.at[slot, o]))
    copies = copy_all(moves, sems)
    for slot in range(2):
        for o in range(2):
            copies[slot * 2 + o].wait()
            for b in range(2):
                for s, mask in enumerate(ring_masks(b)):
                    block = (zl ^ b) * 4 + (y ^ mask)
                    lanes = pl.ds(pl.multiple_of(block * 256 + c * 128, 128), 128)
                    re, im = held[slot, o, 0, :, lanes], held[slot, o, 1, :, lanes]
                    row, col = o * 256, (b * 4 + s) * 256
                    out_ref[slot, row : row + 128, col : col + 128] = re
                    out_ref[slot, row : row + 128, col + 128 : col + 256] = -im
                    out_ref[slot, row + 128 : row + 256, col : col + 128] = im
                    out_ref[slot, row + 128 : row + 256, col + 128 : col + 256] = re


def screen(w_ref, *refs):
    pieces, outs, (acc, held, sems) = refs[:4], refs[4:7], refs[7:]
    copies = copy_all([(ref, held.at[i]) for i, ref in enumerate(pieces)], sems)
    for i in range(8):
        if i % 2 == 0:
            copies[i // 2].wait()
        cols = slice(i * 256, (i + 1) * 256)
        for p, (k, kp) in enumerate(PAIRS):
            rhs = held[i // 2, i % 2, kp].reshape(256, 256)
            term = jnp.dot(w_ref[kp - k, :, cols], rhs, preferred_element_type=F32)
            if i == 0:
                acc[p] = term
            else:
                acc[p] += term
    for p, ref in enumerate(outs):
        ref[...] = acc[p].reshape(2, 2, 128, 256).astype(BF)


def right_side(mine_ref, got_ref):
    blocks = []
    for o in range(2):
        re = (mine_ref[o, 0].astype(F32) + got_ref[1 - o, 0].astype(F32)).astype(BF)
        im = (mine_ref[o, 1].astype(F32) + got_ref[1 - o, 1].astype(F32)).astype(BF)
        blocks += [jnp.concatenate((re, im), 1), jnp.concatenate((im, -re), 1)]
    return jnp.concatenate(blocks, 0)


def rows_for(b, s, k, pieces):
    x, zh, zl, y, c = (lax.axis_index(a) for a in ("x", "zh", "zl", "y", "c"))
    j = (zl ^ b) * 4 + lax.rem(y + s, 4)
    mask = (j // 2) ^ x
    near = (mask == 0) | (mask == 1 + 2 * c)
    unit = jnp.where((mask == 0) | (mask == 3 - 2 * c), 0, 1)
    same = lax.rem(j, 2) == zh
    values = [ref[unit, k] for ref in pieces]
    own = jnp.where(near, values[0], values[1])
    far = jnp.where(near, values[2], values[3])
    return jnp.where(same, own, far)


def contract_y(factor, m0_ref, g0_ref, m1_ref, g1_ref, r0, r1, r2, r3, k_ref, s1_ref, s2_ref, s3_ref, rest_ref):
    rhs = [right_side(m0_ref, g0_ref), right_side(m1_ref, g1_ref)]
    for b in range(2):
        for s, ref in enumerate((k_ref, s1_ref, s2_ref, s3_ref)):
            rows = rows_for(b, s, 0, (r0, r1, r2, r3))
            for p in range(2):
                part = jnp.dot(rows, rhs[p], preferred_element_type=F32)
                part = (part * factor).astype(BF)
                if p == 0:
                    ref[b, :, :512] = part
                else:
                    ref[b, :, 512:] = part[:, :CUT]
                    rest_ref[b, s] = part[:, CUT:]


def contract_z(factor, mine_ref, got_ref, r0, r1, r2, r3, rest_ref, k_ref, s_ref):
    rhs = right_side(mine_ref, got_ref)
    for b, ref in enumerate((k_ref, s_ref)):
        for s in range(4):
            part = jnp.dot(rows_for(b, s, 1, (r0, r1, r2, r3)), rhs, preferred_element_type=F32)
            ref[s, :, :512] = (part * factor).astype(BF)
            ref[s, :, 512:] = rest_ref[b, s]


def add_z(keep_ref, got_ref, *outs):
    for s, ref in enumerate(outs):
        ref[...] = (keep_ref[s].astype(F32) + got_ref[s].astype(F32)).astype(BF)


def add_y(keep_ref, g1_ref, g2_ref, g3_ref, out_ref, send_ref):
    for b, ref in enumerate((out_ref, send_ref)):
        near = keep_ref[b].astype(F32) + g1_ref[b].astype(F32)
        ref[...] = (near + (g2_ref[b].astype(F32) + g3_ref[b].astype(F32))).astype(BF)


def finish(list_ref, z0_ref, z1_ref, z2_ref, z3_ref, y0_ref, y1_ref, out_ref):
    z = z0_ref[...].astype(F32) + z1_ref[...].astype(F32) + (z2_ref[...].astype(F32) + z3_ref[...].astype(F32))
    y = y0_ref[...].astype(F32) + y1_ref[...].astype(F32)
    sums = (y[:, :512], jnp.concatenate((y[:, 512:], z[:, 512:]), 1), z[:, :512])
    for pair, value in zip(PAIRS, sums):
        out_ref[pair_row(list_ref, pair)] = value.astype(BF)


def shift(x, axis, size, step):
    return lax.ppermute(x, axis, [(i, (i + step) % size) for i in range(size)])


def ring_swap(x, axis, second):
    pairs = [(i * 2 + c, (i ^ (3 if c ^ second else 1)) * 2 + c) for i in range(4) for c in range(2)]
    return lax.ppermute(x, (axis, "c"), pairs)


def double(x, got):
    return call(join, [(2,) + x.shape], [ANY] * 2, x, got, scratch=[pltpu.SemaphoreType.DMA((2,))])[0]


def tie(*xs):
    return lax.optimization_barrier(xs)


def per_device(matrix_elements, screening, pair_list, pair_q):
    factor = 1.0 / math.sqrt(2.0 * screening.shape[3])
    m, pairs = matrix_elements, pair_list.T
    mine, other = call(transpose_halves, [(2, 128, 256)] * 2, [VMEM], m)
    (rows,) = call(join_halves, [(2, 128, 512)], [VMEM] * 2, mine, shift(other, "c", 2, 1))
    mate_weights = shift(screening, "c", 2, 1)
    m_far = shift(m, "zl", 2, 1)
    m_got = ring_swap(m, "y", 0)
    rows_far = shift(rows, "zh", 2, 1)
    rows_got = ring_swap(rows, "x", 0)
    m_near = double(m, m_got)
    m_next = ring_swap(m_near, "y", 1)
    rows_near = double(rows, rows_got)
    rows_next = ring_swap(rows_near, "x", 1)
    m_far_got = ring_swap(m_far, "y", 1)
    m_far_got, rows_far = tie(m_far_got, rows_far)
    rows_far_got = ring_swap(rows_far, "x", 0)
    m_far_near = double(m_far, m_far_got)
    m_far_next = ring_swap(m_far_near, "y", 0)
    rows_far_near = double(rows_far, rows_far_got)
    rows_far_next = ring_swap(rows_far_near, "x", 1)
    (weights,) = call(
        weight_rows,
        [(2, 512, 2048)],
        [SMEM] * 2 + [ANY] * 2,
        pairs,
        pair_q,
        screening,
        mate_weights,
        limit=8,
        scratch=[pltpu.VMEM((2, 2, 2, 128, 2048), BF), pltpu.SemaphoreType.DMA((4,))],
    )
    weights, rows_next = tie(weights, rows_next)
    parts = call(
        screen,
        [(2, 2, 128, 256)] * 3,
        [VMEM] + [ANY] * 4,
        weights,
        m_near,
        m_next,
        m_far_near,
        m_far_next,
        limit=8,
        scratch=[pltpu.VMEM((3, 512, 256), F32), pltpu.VMEM((4, 2, 2, 2, 128, 256), BF), pltpu.SemaphoreType.DMA((4,))],
    )
    sides = [(part, shift(part, "c", 2, 1)) for part in parts]
    left = [rows_near, rows_next, rows_far_near, rows_far_next]
    y_keep, y1, y2, y3, rest = call(
        functools.partial(contract_y, factor),
        [(2, 128, WIDE_Y)] * 4 + [(2, 4, 128, 512 - CUT)],
        [VMEM] * 8,
        *sides[0],
        *sides[1],
        *left,
        limit=8,
    )
    z_keep, z_send = call(
        functools.partial(contract_z, factor), [(4, 128, WIDE_Z)] * 2, [VMEM] * 7, *sides[2], *left, rest, limit=8
    )
    z_got = shift(z_send, "zl", 2, 1)
    y_got = [shift(y1, "y", 4, 1), shift(y3, "y", 4, -1), shift(y2, "y", 4, 2)]
    z_sums = call(add_z, [(128, WIDE_Z)] * 4, [VMEM] * 2, z_keep, z_got)
    y_keep, y_send = call(add_y, [(128, WIDE_Y)] * 2, [VMEM] * 4, y_keep, *y_got)
    z_last = [shift(z_sums[1], "y", 4, 1), shift(z_sums[3], "y", 4, -1), shift(z_sums[2], "y", 4, 2)]
    y_last = shift(y_send, "zl", 2, 1)
    (out,) = call(finish, [(3, 128, 512)], [SMEM] + [VMEM] * 6, pairs, z_sums[0], *z_last, y_keep, y_last)
    return out.reshape(3, 128, 2, 256)


def solution(mesh):
    split = Mesh(mesh.devices.reshape(4, 2, 2, 4, 2), ("x", "zh", "zl", "y", "c"))
    ga = ("zl", "y", "c")
    return jax.shard_map(
        per_device,
        mesh=split,
        in_specs=(P(None, None, ga, ("x", "zh")), P(None, None, ga, None), P(), P()),
        out_specs=P(None, ga, None, ("x", "zh")),
        check_vma=False,
    )
```

```python
import functools
import math

import jax
import jax.numpy as jnp
from jax import lax
from jax.experimental import pallas as pl
from jax.experimental.pallas import tpu as pltpu
from jax.sharding import Mesh, PartitionSpec as P

BF = jnp.bfloat16
F32 = jnp.float32
MIB = 1024 * 1024
VMEM = pl.BlockSpec(memory_space=pltpu.VMEM)
SMEM = pl.BlockSpec(memory_space=pltpu.SMEM)
ANY = pl.BlockSpec(memory_space=pl.ANY)
PAIRS = ((0, 0), (0, 1), (1, 1))
CUT = 256
WIDE_Y = 512 + CUT
WIDE_Z = 1024 - CUT


def call(body, outs, specs, *args, scratch=(), limit=2):
    return pl.pallas_call(
        body,
        out_shape=[jax.ShapeDtypeStruct(s, BF) for s in outs],
        in_specs=specs,
        out_specs=[VMEM] * len(outs),
        scratch_shapes=list(scratch),
        compiler_params=pltpu.CompilerParams(vmem_limit_bytes=limit * MIB),
    )(*args)


def copy_all(moves, sems):
    copies = [pltpu.make_async_copy(src, dst, sems.at[i]) for i, (src, dst) in enumerate(moves)]
    for copy in copies:
        copy.start()
    return copies


def transpose_halves(m_ref, mine_ref, other_ref):
    c = lax.axis_index("c")
    for k in range(2):
        for part in range(2):
            lanes = slice(part * 128, (part + 1) * 128)
            mine_ref[k, :, lanes] = m_ref[k, part, :, pl.ds(pl.multiple_of(c * 128, 128), 128)].T
            other_ref[k, :, lanes] = m_ref[k, part, :, pl.ds(pl.multiple_of((1 - c) * 128, 128), 128)].T


def join_halves(mine_ref, got_ref, out_ref):
    out_ref[:, :, :256] = mine_ref[...]
    out_ref[:, :, 256:] = got_ref[...]


def join(a_ref, b_ref, out_ref, sems):
    for copy in copy_all([(a_ref, out_ref.at[0]), (b_ref, out_ref.at[1])], sems):
        copy.wait()


def ring_masks(flip=0):
    c = lax.axis_index("c")
    c = 1 - c if flip else c
    return (0, 1 + 2 * c, 3 - 2 * c, 2)


def pair_row(list_ref, pair):
    row = 0
    for r in range(1, 3):
        row = jnp.where((list_ref[0, r] == pair[0]) & (list_ref[1, r] == pair[1]), r, row)
    return row


def weight_rows(list_ref, q_ref, own_ref, mate_ref, out_ref, held, sems):
    zl, y, c = lax.axis_index("zl"), lax.axis_index("y"), lax.axis_index("c")
    moves = []
    for slot in range(2):
        q = q_ref[pair_row(list_ref, PAIRS[slot])]
        for o, ref in enumerate((own_ref, mate_ref)):
            moves.append((ref.at[q], held.at[slot, o]))
    copies = copy_all(moves, sems)
    for slot in range(2):
        for o in range(2):
            copies[slot * 2 + o].wait()
            for b in range(2):
                for s, mask in enumerate(ring_masks(b)):
                    block = (zl ^ b) * 4 + (y ^ mask)
                    lanes = pl.ds(pl.multiple_of(block * 256 + c * 128, 128), 128)
                    re, im = held[slot, o, 0, :, lanes], held[slot, o, 1, :, lanes]
                    row, col = o * 256, (b * 4 + s) * 256
                    out_ref[slot, row : row + 128, col : col + 128] = re
                    out_ref[slot, row : row + 128, col + 128 : col + 256] = -im
                    out_ref[slot, row + 128 : row + 256, col : col + 128] = im
                    out_ref[slot, row + 128 : row + 256, col + 128 : col + 256] = re


def screen(w_ref, *refs):
    pieces, outs, (acc, held, sems) = refs[:4], refs[4:7], refs[7:]
    copies = copy_all([(ref, held.at[i]) for i, ref in enumerate(pieces)], sems)
    for i in range(8):
        if i % 2 == 0:
            copies[i // 2].wait()
        cols = slice(i * 256, (i + 1) * 256)
        for p, (k, kp) in enumerate(PAIRS):
            rhs = held[i // 2, i % 2, kp].reshape(256, 256)
            term = jnp.dot(w_ref[kp - k, :, cols], rhs, preferred_element_type=F32)
            if i == 0:
                acc[p] = term
            else:
                acc[p] += term
    for p, ref in enumerate(outs):
        ref[...] = acc[p].reshape(2, 2, 128, 256).astype(BF)


def right_side(mine_ref, got_ref):
    blocks = []
    for o in range(2):
        re = (mine_ref[o, 0].astype(F32) + got_ref[1 - o, 0].astype(F32)).astype(BF)
        im = (mine_ref[o, 1].astype(F32) + got_ref[1 - o, 1].astype(F32)).astype(BF)
        blocks += [jnp.concatenate((re, im), 1), jnp.concatenate((im, -re), 1)]
    return jnp.concatenate(blocks, 0)


def rows_for(b, s, k, pieces):
    x, zh, zl, y, c = (lax.axis_index(a) for a in ("x", "zh", "zl", "y", "c"))
    j = (zl ^ b) * 4 + lax.rem(y + s, 4)
    mask = (j // 2) ^ x
    same = lax.rem(j, 2) == zh
    first = jnp.where(same, 1 + 2 * c, 3 - 2 * c)
    near = (mask == 0) | (mask == first)
    unit = jnp.where((mask == 0) | (mask == 4 - first), 0, 1)
    values = [ref[unit, k] for ref in pieces]
    own = jnp.where(near, values[0], values[1])
    far = jnp.where(near, values[2], values[3])
    return jnp.where(same, own, far)


def contract_y(factor, m0_ref, g0_ref, m1_ref, g1_ref, r0, r1, r2, r3, k_ref, s1_ref, s2_ref, s3_ref, rest_ref):
    rhs = [right_side(m0_ref, g0_ref), right_side(m1_ref, g1_ref)]
    for b in range(2):
        for s, ref in enumerate((k_ref, s1_ref, s2_ref, s3_ref)):
            rows = rows_for(b, s, 0, (r0, r1, r2, r3))
            for p in range(2):
                part = jnp.dot(rows, rhs[p], preferred_element_type=F32)
                part = (part * factor).astype(BF)
                if p == 0:
                    ref[b, :, :512] = part
                else:
                    ref[b, :, 512:] = part[:, :CUT]
                    rest_ref[b, s] = part[:, CUT:]


def contract_z(factor, mine_ref, got_ref, r0, r1, r2, r3, rest_ref, k_ref, s_ref):
    rhs = right_side(mine_ref, got_ref)
    for b, ref in enumerate((k_ref, s_ref)):
        for s in range(4):
            part = jnp.dot(rows_for(b, s, 1, (r0, r1, r2, r3)), rhs, preferred_element_type=F32)
            ref[s, :, :512] = (part * factor).astype(BF)
            ref[s, :, 512:] = rest_ref[b, s]


def add_z(keep_ref, got_ref, *outs):
    for s, ref in enumerate(outs):
        ref[...] = (keep_ref[s].astype(F32) + got_ref[s].astype(F32)).astype(BF)


def add_y(keep_ref, g1_ref, g2_ref, g3_ref, after_ref, out_ref, send_ref):
    for b, ref in enumerate((out_ref, send_ref)):
        near = keep_ref[b].astype(F32) + g1_ref[b].astype(F32)
        ref[...] = (near + (g2_ref[b].astype(F32) + g3_ref[b].astype(F32))).astype(BF)


def finish(list_ref, z0_ref, z1_ref, z2_ref, z3_ref, y0_ref, y1_ref, out_ref):
    z = z0_ref[...].astype(F32) + z1_ref[...].astype(F32) + (z2_ref[...].astype(F32) + z3_ref[...].astype(F32))
    y = y0_ref[...].astype(F32) + y1_ref[...].astype(F32)
    sums = (y[:, :512], jnp.concatenate((y[:, 512:], z[:, 512:]), 1), z[:, :512])
    for pair, value in zip(PAIRS, sums):
        out_ref[pair_row(list_ref, pair)] = value.astype(BF)


def shift(x, axis, size, step):
    return lax.ppermute(x, axis, [(i, (i + step) % size) for i in range(size)])


def ring_swap(x, axis, second):
    pairs = [(i * 2 + c, (i ^ (3 if c ^ second else 1)) * 2 + c) for i in range(4) for c in range(2)]
    return lax.ppermute(x, (axis, "c"), pairs)


def double(x, got):
    return call(join, [(2,) + x.shape], [ANY] * 2, x, got, scratch=[pltpu.SemaphoreType.DMA((2,))])[0]


def tie(*xs):
    return lax.optimization_barrier(xs)


def per_device(matrix_elements, screening, pair_list, pair_q):
    factor = 1.0 / math.sqrt(2.0 * screening.shape[3])
    m, pairs = matrix_elements, pair_list.T
    mine, other = call(transpose_halves, [(2, 128, 256)] * 2, [VMEM], m)
    (rows,) = call(join_halves, [(2, 128, 512)], [VMEM] * 2, mine, shift(other, "c", 2, 1))
    mate_weights = shift(screening, "c", 2, 1)
    m_far = shift(m, "zl", 2, 1)
    m_got = ring_swap(m, "y", 0)
    rows_far = shift(rows, "zh", 2, 1)
    rows_got = ring_swap(rows, "x", 0)
    m_near = double(m, m_got)
    m_next = ring_swap(m_near, "y", 1)
    rows_near = double(rows, rows_got)
    rows_next = ring_swap(rows_near, "x", 1)
    m_far_got = ring_swap(m_far, "y", 1)
    m_far_got, rows_far = tie(m_far_got, rows_far)
    rows_far_got = ring_swap(rows_far, "x", 1)
    m_far_near = double(m_far, m_far_got)
    m_far_next = ring_swap(m_far_near, "y", 0)
    rows_far_near = double(rows_far, rows_far_got)
    rows_far_next = ring_swap(rows_far_near, "x", 0)
    (weights,) = call(
        weight_rows,
        [(2, 512, 2048)],
        [SMEM] * 2 + [ANY] * 2,
        pairs,
        pair_q,
        screening,
        mate_weights,
        limit=8,
        scratch=[pltpu.VMEM((2, 2, 2, 128, 2048), BF), pltpu.SemaphoreType.DMA((4,))],
    )
    weights, rows_next = tie(weights, rows_next)
    parts = call(
        screen,
        [(2, 2, 128, 256)] * 3,
        [VMEM] + [ANY] * 4,
        weights,
        m_near,
        m_next,
        m_far_near,
        m_far_next,
        limit=8,
        scratch=[pltpu.VMEM((3, 512, 256), F32), pltpu.VMEM((4, 2, 2, 2, 128, 256), BF), pltpu.SemaphoreType.DMA((4,))],
    )
    sides = [(part, shift(part, "c", 2, 1)) for part in parts]
    left = [rows_near, rows_next, rows_far_near, rows_far_next]
    y_keep, y1, y2, y3, rest = call(
        functools.partial(contract_y, factor),
        [(2, 128, WIDE_Y)] * 4 + [(2, 4, 128, 512 - CUT)],
        [VMEM] * 8,
        *sides[0],
        *sides[1],
        *left,
        limit=8,
    )
    z_keep, z_send = call(
        functools.partial(contract_z, factor), [(4, 128, WIDE_Z)] * 2, [VMEM] * 7, *sides[2], *left, rest, limit=8
    )
    z_got = shift(z_send, "zl", 2, 1)
    y_got = [shift(y1, "y", 4, 1), shift(y3, "y", 4, -1), shift(y2, "y", 4, 2)]
    z_sums = call(add_z, [(128, WIDE_Z)] * 4, [VMEM] * 2, z_keep, z_got)
    y_keep, y_send = call(add_y, [(128, WIDE_Y)] * 2, [VMEM] * 4 + [ANY], y_keep, *y_got, z_sums[0])
    z_last = [shift(z_sums[1], "y", 4, 1), shift(z_sums[3], "y", 4, -1), shift(z_sums[2], "y", 4, 2)]
    y_last = shift(y_send, "zl", 2, 1)
    (out,) = call(finish, [(3, 128, 512)], [SMEM] + [VMEM] * 6, pairs, z_sums[0], *z_last, y_keep, y_last)
    return out.reshape(3, 128, 2, 256)


def solution(mesh):
    split = Mesh(mesh.devices.reshape(4, 2, 2, 4, 2), ("x", "zh", "zl", "y", "c"))
    ga = ("zl", "y", "c")
    return jax.shard_map(
        per_device,
        mesh=split,
        in_specs=(P(None, None, ga, ("x", "zh")), P(None, None, ga, None), P(), P()),
        out_specs=P(None, ga, None, ("x", "zh")),
        check_vma=False,
    )
```

```python
import functools
import math

import jax
import jax.numpy as jnp
from jax import lax
from jax.experimental import pallas as pl
from jax.experimental.pallas import tpu as pltpu
from jax.sharding import Mesh, PartitionSpec as P

BF = jnp.bfloat16
F32 = jnp.float32
MIB = 1024 * 1024
VMEM = pl.BlockSpec(memory_space=pltpu.VMEM)
SMEM = pl.BlockSpec(memory_space=pltpu.SMEM)
ANY = pl.BlockSpec(memory_space=pl.ANY)
PAIRS = ((0, 0), (0, 1), (1, 1))
CUT = 256
WIDE_Y = 512 + CUT
WIDE_Z = 1024 - CUT


def call(body, outs, specs, *args, scratch=(), limit=2):
    return pl.pallas_call(
        body,
        out_shape=[jax.ShapeDtypeStruct(s, BF) for s in outs],
        in_specs=specs,
        out_specs=[VMEM] * len(outs),
        scratch_shapes=list(scratch),
        compiler_params=pltpu.CompilerParams(vmem_limit_bytes=limit * MIB),
    )(*args)


def copy_all(moves, sems):
    copies = [pltpu.make_async_copy(src, dst, sems.at[i]) for i, (src, dst) in enumerate(moves)]
    for copy in copies:
        copy.start()
    return copies


def transpose_halves(m_ref, mine_ref, other_ref):
    c = lax.axis_index("c")
    for k in range(2):
        for part in range(2):
            lanes = slice(part * 128, (part + 1) * 128)
            mine_ref[k, :, lanes] = m_ref[k, part, :, pl.ds(pl.multiple_of(c * 128, 128), 128)].T
            other_ref[k, :, lanes] = m_ref[k, part, :, pl.ds(pl.multiple_of((1 - c) * 128, 128), 128)].T


def join_halves(mine_ref, got_ref, out_ref):
    out_ref[:, :, :256] = mine_ref[...]
    out_ref[:, :, 256:] = got_ref[...]


def join(a_ref, b_ref, out_ref, sems):
    for copy in copy_all([(a_ref, out_ref.at[0]), (b_ref, out_ref.at[1])], sems):
        copy.wait()


def ring_masks(flip=0):
    c = lax.axis_index("c")
    c = 1 - c if flip else c
    return (0, 1 + 2 * c, 3 - 2 * c, 2)


def pair_row(list_ref, pair):
    row = 0
    for r in range(1, 3):
        row = jnp.where((list_ref[0, r] == pair[0]) & (list_ref[1, r] == pair[1]), r, row)
    return row


def weight_rows(list_ref, q_ref, own_ref, mate_ref, out_ref, held, sems):
    zl, y, c = lax.axis_index("zl"), lax.axis_index("y"), lax.axis_index("c")
    moves = []
    for slot in range(2):
        q = q_ref[pair_row(list_ref, PAIRS[slot])]
        for o, ref in enumerate((own_ref, mate_ref)):
            moves.append((ref.at[q], held.at[slot, o]))
    copies = copy_all(moves, sems)
    for slot in range(2):
        for o in range(2):
            copies[slot * 2 + o].wait()
            for b in range(2):
                for s, mask in enumerate(ring_masks(b)):
                    block = (zl ^ b) * 4 + (y ^ mask)
                    lanes = pl.ds(pl.multiple_of(block * 256 + c * 128, 128), 128)
                    re, im = held[slot, o, 0, :, lanes], held[slot, o, 1, :, lanes]
                    row, col = o * 256, (b * 4 + s) * 256
                    out_ref[slot, row : row + 128, col : col + 128] = re
                    out_ref[slot, row : row + 128, col + 128 : col + 256] = -im
                    out_ref[slot, row + 128 : row + 256, col : col + 128] = im
                    out_ref[slot, row + 128 : row + 256, col + 128 : col + 256] = re


def screen(w_ref, *refs):
    pieces, outs, (acc, held, sems) = refs[:4], refs[4:7], refs[7:]
    copies = copy_all([(ref, held.at[i]) for i, ref in enumerate(pieces)], sems)
    for i in range(8):
        if i % 2 == 0:
            copies[i // 2].wait()
        cols = slice(i * 256, (i + 1) * 256)
        for p, (k, kp) in enumerate(PAIRS):
            rhs = held[i // 2, i % 2, kp].reshape(256, 256)
            term = jnp.dot(w_ref[kp - k, :, cols], rhs, preferred_element_type=F32)
            if i == 0:
                acc[p] = term
            else:
                acc[p] += term
    for p, ref in enumerate(outs):
        ref[...] = acc[p].reshape(2, 2, 128, 256).astype(BF)


def right_side(mine_ref, got_ref):
    blocks = []
    for o in range(2):
        re = (mine_ref[o, 0].astype(F32) + got_ref[1 - o, 0].astype(F32)).astype(BF)
        im = (mine_ref[o, 1].astype(F32) + got_ref[1 - o, 1].astype(F32)).astype(BF)
        blocks += [jnp.concatenate((re, im), 1), jnp.concatenate((im, -re), 1)]
    return jnp.concatenate(blocks, 0)


def rows_for(b, s, k, pieces):
    x, zh, zl, y, c = (lax.axis_index(a) for a in ("x", "zh", "zl", "y", "c"))
    j = (zl ^ b) * 4 + lax.rem(y + s, 4)
    mask = (j // 2) ^ x
    same = lax.rem(j, 2) == zh
    first = jnp.where(same, 1 + 2 * c, 3 - 2 * c)
    near = (mask == 0) | (mask == first)
    unit = jnp.where((mask == 0) | (mask == 4 - first), 0, 1)
    values = [ref[unit, k] for ref in pieces]
    own = jnp.where(near, values[0], values[1])
    far = jnp.where(near, values[2], values[3])
    return jnp.where(same, own, far)


def contract_y(factor, m0_ref, g0_ref, m1_ref, g1_ref, r0, r1, r2, r3, k_ref, s1_ref, s2_ref, s3_ref, rest_ref):
    rhs = [right_side(m0_ref, g0_ref), right_side(m1_ref, g1_ref)]
    for b in range(2):
        for s, ref in enumerate((k_ref, s1_ref, s2_ref, s3_ref)):
            rows = rows_for(b, s, 0, (r0, r1, r2, r3))
            for p in range(2):
                part = jnp.dot(rows, rhs[p], preferred_element_type=F32)
                part = (part * factor).astype(BF)
                if p == 0:
                    ref[b, :, :512] = part
                else:
                    ref[b, :, 512:] = part[:, :CUT]
                    rest_ref[b, s] = part[:, CUT:]


def contract_z(factor, mine_ref, got_ref, r0, r1, r2, r3, rest_ref, k_ref, s_ref):
    rhs = right_side(mine_ref, got_ref)
    for b, ref in enumerate((k_ref, s_ref)):
        for s in range(4):
            part = jnp.dot(rows_for(b, s, 1, (r0, r1, r2, r3)), rhs, preferred_element_type=F32)
            ref[s, :, :512] = (part * factor).astype(BF)
            ref[s, :, 512:] = rest_ref[b, s]


def add_z(keep_ref, got_ref, *outs):
    for s, ref in enumerate(outs):
        ref[...] = (keep_ref[s].astype(F32) + got_ref[s].astype(F32)).astype(BF)


def add_y(keep_ref, g1_ref, g2_ref, g3_ref, after_ref, out_ref, send_ref):
    for b, ref in enumerate((out_ref, send_ref)):
        near = keep_ref[b].astype(F32) + g1_ref[b].astype(F32)
        ref[...] = (near + (g2_ref[b].astype(F32) + g3_ref[b].astype(F32))).astype(BF)


def finish(list_ref, z0_ref, z1_ref, z2_ref, z3_ref, y0_ref, y1_ref, out_ref):
    z = z0_ref[...].astype(F32) + z1_ref[...].astype(F32) + (z2_ref[...].astype(F32) + z3_ref[...].astype(F32))
    y = y0_ref[...].astype(F32) + y1_ref[...].astype(F32)
    sums = (y[:, :512], jnp.concatenate((y[:, 512:], z[:, 512:]), 1), z[:, :512])
    for pair, value in zip(PAIRS, sums):
        out_ref[pair_row(list_ref, pair)] = value.astype(BF)


def shift(x, axis, size, step):
    return lax.ppermute(x, axis, [(i, (i + step) % size) for i in range(size)])


def ring_swap(x, axis, second):
    pairs = [(i * 2 + c, (i ^ (3 if c ^ second else 1)) * 2 + c) for i in range(4) for c in range(2)]
    return lax.ppermute(x, (axis, "c"), pairs)


def double(x, got):
    return call(join, [(2,) + x.shape], [ANY] * 2, x, got, scratch=[pltpu.SemaphoreType.DMA((2,))])[0]


def tie(*xs):
    return lax.optimization_barrier(xs)


def per_device(matrix_elements, screening, pair_list, pair_q):
    factor = 1.0 / math.sqrt(2.0 * screening.shape[3])
    m, pairs = matrix_elements, pair_list.T
    mine, other = call(transpose_halves, [(2, 128, 256)] * 2, [VMEM], m)
    (rows,) = call(join_halves, [(2, 128, 512)], [VMEM] * 2, mine, shift(other, "c", 2, 1))
    mate_weights = shift(screening, "c", 2, 1)
    m_far = shift(m, "zl", 2, 1)
    m_got = ring_swap(m, "y", 0)
    rows_far = shift(rows, "zh", 2, 1)
    rows_got = ring_swap(rows, "x", 0)
    m_near = double(m, m_got)
    m_next = ring_swap(m_near, "y", 1)
    rows_near = double(rows, rows_got)
    rows_next = ring_swap(rows_near, "x", 1)
    m_far_got = ring_swap(m_far, "y", 1)
    m_far_got, rows_far = tie(m_far_got, rows_far)
    rows_far_got = ring_swap(rows_far, "x", 1)
    m_far_near = double(m_far, m_far_got)
    m_far_next = ring_swap(m_far_near, "y", 0)
    rows_far_near = double(rows_far, rows_far_got)
    rows_far_next = ring_swap(rows_far_near, "x", 0)
    (weights,) = call(
        weight_rows,
        [(2, 512, 2048)],
        [SMEM] * 2 + [ANY] * 2,
        pairs,
        pair_q,
        screening,
        mate_weights,
        limit=8,
        scratch=[pltpu.VMEM((2, 2, 2, 128, 2048), BF), pltpu.SemaphoreType.DMA((4,))],
    )
    weights, rows_next = tie(weights, rows_next)
    parts = call(
        screen,
        [(2, 2, 128, 256)] * 3,
        [VMEM] + [ANY] * 4,
        weights,
        m_near,
        m_next,
        m_far_near,
        m_far_next,
        limit=8,
        scratch=[pltpu.VMEM((3, 512, 256), F32), pltpu.VMEM((4, 2, 2, 2, 128, 256), BF), pltpu.SemaphoreType.DMA((4,))],
    )
    sides = [(part, shift(part, "c", 2, 1)) for part in parts]
    left = [rows_near, rows_next, rows_far_near, rows_far_next]
    y_keep, y1, y2, y3, rest = call(
        functools.partial(contract_y, factor),
        [(2, 128, WIDE_Y)] * 4 + [(2, 4, 128, 512 - CUT)],
        [VMEM] * 8,
        *sides[0],
        *sides[1],
        *left,
        limit=8,
    )
    z_keep, z_send = call(
        functools.partial(contract_z, factor), [(4, 128, WIDE_Z)] * 2, [VMEM] * 7, *sides[2], *left, rest, limit=8
    )
    z_got = shift(z_send, "zl", 2, 1)
    y_got = [shift(y1, "y", 4, 1), shift(y3, "y", 4, -1), shift(y2, "y", 4, 2)]
    z_sums = call(add_z, [(128, WIDE_Z)] * 4, [VMEM] * 2, z_keep, z_got)
    y_keep, y_send = call(add_y, [(128, WIDE_Y)] * 2, [VMEM] * 4 + [ANY], y_keep, *y_got, z_sums[0])
    z_last = [shift(z_sums[2], "y", 4, 2), shift(z_sums[1], "y", 4, 1), shift(z_sums[3], "y", 4, -1)]
    y_last = shift(y_send, "zl", 2, 1)
    (out,) = call(finish, [(3, 128, 512)], [SMEM] + [VMEM] * 6, pairs, z_sums[0], *z_last, y_keep, y_last)
    return out.reshape(3, 128, 2, 256)


def solution(mesh):
    split = Mesh(mesh.devices.reshape(4, 2, 2, 4, 2), ("x", "zh", "zl", "y", "c"))
    ga = ("zl", "y", "c")
    return jax.shard_map(
        per_device,
        mesh=split,
        in_specs=(P(None, None, ga, ("x", "zh")), P(None, None, ga, None), P(), P()),
        out_specs=P(None, ga, None, ("x", "zh")),
        check_vma=False,
    )
```

```python
import functools
import math

import jax
import jax.numpy as jnp
from jax import lax
from jax.experimental import pallas as pl
from jax.experimental.pallas import tpu as pltpu
from jax.sharding import Mesh, PartitionSpec as P

BF = jnp.bfloat16
F32 = jnp.float32
MIB = 1024 * 1024
VMEM = pl.BlockSpec(memory_space=pltpu.VMEM)
SMEM = pl.BlockSpec(memory_space=pltpu.SMEM)
ANY = pl.BlockSpec(memory_space=pl.ANY)
PAIRS = ((0, 0), (0, 1), (1, 1))
CUT = 256
WIDE_Y = 512 + CUT
WIDE_Z = 1024 - CUT


def call(body, outs, specs, *args, scratch=(), limit=2):
    return pl.pallas_call(
        body,
        out_shape=[jax.ShapeDtypeStruct(s, BF) for s in outs],
        in_specs=specs,
        out_specs=[VMEM] * len(outs),
        scratch_shapes=list(scratch),
        compiler_params=pltpu.CompilerParams(vmem_limit_bytes=limit * MIB),
    )(*args)


def copy_all(moves, sems):
    copies = [pltpu.make_async_copy(src, dst, sems.at[i]) for i, (src, dst) in enumerate(moves)]
    for copy in copies:
        copy.start()
    return copies


def transpose_halves(m_ref, mine_ref, other_ref):
    c = lax.axis_index("c")
    for k in range(2):
        for part in range(2):
            lanes = slice(part * 128, (part + 1) * 128)
            mine_ref[k, :, lanes] = m_ref[k, part, :, pl.ds(pl.multiple_of(c * 128, 128), 128)].T
            other_ref[k, :, lanes] = m_ref[k, part, :, pl.ds(pl.multiple_of((1 - c) * 128, 128), 128)].T


def join_halves(mine_ref, got_ref, out_ref):
    out_ref[:, :, :256] = mine_ref[...]
    out_ref[:, :, 256:] = got_ref[...]


def join(a_ref, b_ref, out_ref, sems):
    for copy in copy_all([(a_ref, out_ref.at[0]), (b_ref, out_ref.at[1])], sems):
        copy.wait()


def ring_masks(flip=0):
    c = lax.axis_index("c")
    c = 1 - c if flip else c
    return (0, 1 + 2 * c, 3 - 2 * c, 2)


def pair_row(list_ref, pair):
    row = 0
    for r in range(1, 3):
        row = jnp.where((list_ref[0, r] == pair[0]) & (list_ref[1, r] == pair[1]), r, row)
    return row


def weight_rows(list_ref, q_ref, own_ref, mate_ref, out_ref, held, sems):
    zl, y, c = lax.axis_index("zl"), lax.axis_index("y"), lax.axis_index("c")
    moves = []
    for slot in range(2):
        q = q_ref[pair_row(list_ref, PAIRS[slot])]
        for o, ref in enumerate((own_ref, mate_ref)):
            moves.append((ref.at[q], held.at[slot, o]))
    copies = copy_all(moves, sems)
    for slot in range(2):
        for o in range(2):
            copies[slot * 2 + o].wait()
            for b in range(2):
                for s, mask in enumerate(ring_masks(b)):
                    block = (zl ^ b) * 4 + (y ^ mask)
                    lanes = pl.ds(pl.multiple_of(block * 256 + c * 128, 128), 128)
                    re, im = held[slot, o, 0, :, lanes], held[slot, o, 1, :, lanes]
                    row, col = o * 256, (b * 4 + s) * 256
                    out_ref[slot, row : row + 128, col : col + 128] = re
                    out_ref[slot, row : row + 128, col + 128 : col + 256] = -im
                    out_ref[slot, row + 128 : row + 256, col : col + 128] = im
                    out_ref[slot, row + 128 : row + 256, col + 128 : col + 256] = re


def screen(w_ref, *refs):
    pieces, outs, (acc, held, sems) = refs[:4], refs[4:7], refs[7:]
    copies = copy_all([(ref, held.at[i]) for i, ref in enumerate(pieces)], sems)
    for i in range(4):
        copies[i].wait()
        cols = slice(i * 512, (i + 1) * 512)
        for p, (k, kp) in enumerate(PAIRS):
            rhs = held[i, :, kp].reshape(512, 256)
            term = jnp.dot(w_ref[kp - k, :, cols], rhs, preferred_element_type=F32)
            if i == 0:
                acc[p] = term
            else:
                acc[p] += term
    for p, ref in enumerate(outs):
        ref[...] = acc[p].reshape(2, 2, 128, 256).astype(BF)


def right_side(mine_ref, got_ref):
    blocks = []
    for o in range(2):
        re = (mine_ref[o, 0].astype(F32) + got_ref[1 - o, 0].astype(F32)).astype(BF)
        im = (mine_ref[o, 1].astype(F32) + got_ref[1 - o, 1].astype(F32)).astype(BF)
        blocks += [jnp.concatenate((re, im), 1), jnp.concatenate((im, -re), 1)]
    return jnp.concatenate(blocks, 0)


def rows_for(b, s, k, pieces):
    x, zh, zl, y, c = (lax.axis_index(a) for a in ("x", "zh", "zl", "y", "c"))
    j = (zl ^ b) * 4 + lax.rem(y + s, 4)
    mask = (j // 2) ^ x
    same = lax.rem(j, 2) == zh
    first = jnp.where(same, 1 + 2 * c, 3 - 2 * c)
    near = (mask == 0) | (mask == first)
    unit = jnp.where((mask == 0) | (mask == 4 - first), 0, 1)
    values = [ref[unit, k] for ref in pieces]
    own = jnp.where(near, values[0], values[1])
    far = jnp.where(near, values[2], values[3])
    return jnp.where(same, own, far)


def contract_y(factor, m0_ref, g0_ref, m1_ref, g1_ref, r0, r1, r2, r3, k_ref, s1_ref, s2_ref, s3_ref, rest_ref):
    rhs = [right_side(m0_ref, g0_ref), right_side(m1_ref, g1_ref)]
    for b in range(2):
        for s, ref in enumerate((k_ref, s1_ref, s2_ref, s3_ref)):
            rows = rows_for(b, s, 0, (r0, r1, r2, r3))
            for p in range(2):
                part = jnp.dot(rows, rhs[p], preferred_element_type=F32)
                part = (part * factor).astype(BF)
                if p == 0:
                    ref[b, :, :512] = part
                else:
                    ref[b, :, 512:] = part[:, :CUT]
                    rest_ref[b, s] = part[:, CUT:]


def contract_z(factor, mine_ref, got_ref, r0, r1, r2, r3, rest_ref, k_ref, s_ref):
    rhs = right_side(mine_ref, got_ref)
    for b, ref in enumerate((k_ref, s_ref)):
        for s in range(4):
            part = jnp.dot(rows_for(b, s, 1, (r0, r1, r2, r3)), rhs, preferred_element_type=F32)
            ref[s, :, :512] = (part * factor).astype(BF)
            ref[s, :, 512:] = rest_ref[b, s]


def add_z(keep_ref, got_ref, *outs):
    for s, ref in enumerate(outs):
        ref[...] = (keep_ref[s].astype(F32) + got_ref[s].astype(F32)).astype(BF)


def add_y(keep_ref, g1_ref, g2_ref, g3_ref, after_ref, out_ref, send_ref):
    for b, ref in enumerate((out_ref, send_ref)):
        near = keep_ref[b].astype(F32) + g1_ref[b].astype(F32)
        ref[...] = (near + (g2_ref[b].astype(F32) + g3_ref[b].astype(F32))).astype(BF)


def finish(list_ref, z0_ref, z1_ref, z2_ref, z3_ref, y0_ref, y1_ref, out_ref):
    z = z0_ref[...].astype(F32) + z1_ref[...].astype(F32) + (z2_ref[...].astype(F32) + z3_ref[...].astype(F32))
    y = y0_ref[...].astype(F32) + y1_ref[...].astype(F32)
    sums = (y[:, :512], jnp.concatenate((y[:, 512:], z[:, 512:]), 1), z[:, :512])
    for pair, value in zip(PAIRS, sums):
        out_ref[pair_row(list_ref, pair)] = value.astype(BF)


def shift(x, axis, size, step):
    return lax.ppermute(x, axis, [(i, (i + step) % size) for i in range(size)])


def ring_swap(x, axis, second):
    pairs = [(i * 2 + c, (i ^ (3 if c ^ second else 1)) * 2 + c) for i in range(4) for c in range(2)]
    return lax.ppermute(x, (axis, "c"), pairs)


def double(x, got):
    return call(join, [(2,) + x.shape], [ANY] * 2, x, got, scratch=[pltpu.SemaphoreType.DMA((2,))])[0]


def tie(*xs):
    return lax.optimization_barrier(xs)


def per_device(matrix_elements, screening, pair_list, pair_q):
    factor = 1.0 / math.sqrt(2.0 * screening.shape[3])
    m, pairs = matrix_elements, pair_list.T
    mine, other = call(transpose_halves, [(2, 128, 256)] * 2, [VMEM], m)
    (rows,) = call(join_halves, [(2, 128, 512)], [VMEM] * 2, mine, shift(other, "c", 2, 1))
    mate_weights = shift(screening, "c", 2, 1)
    m_far = shift(m, "zl", 2, 1)
    m_got = ring_swap(m, "y", 0)
    rows_far = shift(rows, "zh", 2, 1)
    rows_got = ring_swap(rows, "x", 0)
    m_near = double(m, m_got)
    m_next = ring_swap(m_near, "y", 1)
    rows_near = double(rows, rows_got)
    rows_next = ring_swap(rows_near, "x", 1)
    m_far_got = ring_swap(m_far, "y", 1)
    m_far_got, rows_far = tie(m_far_got, rows_far)
    rows_far_got = ring_swap(rows_far, "x", 1)
    m_far_near = double(m_far, m_far_got)
    m_far_next = ring_swap(m_far_near, "y", 0)
    rows_far_near = double(rows_far, rows_far_got)
    rows_far_next = ring_swap(rows_far_near, "x", 0)
    (weights,) = call(
        weight_rows,
        [(2, 512, 2048)],
        [SMEM] * 2 + [ANY] * 2,
        pairs,
        pair_q,
        screening,
        mate_weights,
        limit=8,
        scratch=[pltpu.VMEM((2, 2, 2, 128, 2048), BF), pltpu.SemaphoreType.DMA((4,))],
    )
    weights, rows_next = tie(weights, rows_next)
    parts = call(
        screen,
        [(2, 2, 128, 256)] * 3,
        [VMEM] + [ANY] * 4,
        weights,
        m_near,
        m_next,
        m_far_near,
        m_far_next,
        limit=8,
        scratch=[pltpu.VMEM((3, 512, 256), F32), pltpu.VMEM((4, 2, 2, 2, 128, 256), BF), pltpu.SemaphoreType.DMA((4,))],
    )
    sides = [(part, shift(part, "c", 2, 1)) for part in parts]
    left = [rows_near, rows_next, rows_far_near, rows_far_next]
    y_keep, y1, y2, y3, rest = call(
        functools.partial(contract_y, factor),
        [(2, 128, WIDE_Y)] * 4 + [(2, 4, 128, 512 - CUT)],
        [VMEM] * 8,
        *sides[0],
        *sides[1],
        *left,
        limit=8,
    )
    z_keep, z_send = call(
        functools.partial(contract_z, factor), [(4, 128, WIDE_Z)] * 2, [VMEM] * 7, *sides[2], *left, rest, limit=8
    )
    z_got = shift(z_send, "zl", 2, 1)
    y_got = [shift(y1, "y", 4, 1), shift(y3, "y", 4, -1), shift(y2, "y", 4, 2)]
    z_sums = call(add_z, [(128, WIDE_Z)] * 4, [VMEM] * 2, z_keep, z_got)
    y_keep, y_send = call(add_y, [(128, WIDE_Y)] * 2, [VMEM] * 4 + [ANY], y_keep, *y_got, z_sums[0])
    z_last = [shift(z_sums[2], "y", 4, 2), shift(z_sums[1], "y", 4, 1), shift(z_sums[3], "y", 4, -1)]
    y_last = shift(y_send, "zl", 2, 1)
    (out,) = call(finish, [(3, 128, 512)], [SMEM] + [VMEM] * 6, pairs, z_sums[0], *z_last, y_keep, y_last)
    return out.reshape(3, 128, 2, 256)


def solution(mesh):
    split = Mesh(mesh.devices.reshape(4, 2, 2, 4, 2), ("x", "zh", "zl", "y", "c"))
    ga = ("zl", "y", "c")
    return jax.shard_map(
        per_device,
        mesh=split,
        in_specs=(P(None, None, ga, ("x", "zh")), P(None, None, ga, None), P(), P()),
        out_specs=P(None, ga, None, ("x", "zh")),
        check_vma=False,
    )
```

```python
import functools
import math

import jax
import jax.numpy as jnp
from jax import lax
from jax.experimental import pallas as pl
from jax.experimental.pallas import tpu as pltpu
from jax.sharding import Mesh, PartitionSpec as P

BF = jnp.bfloat16
F32 = jnp.float32
MIB = 1024 * 1024
VMEM = pl.BlockSpec(memory_space=pltpu.VMEM)
SMEM = pl.BlockSpec(memory_space=pltpu.SMEM)
ANY = pl.BlockSpec(memory_space=pl.ANY)
PAIRS = ((0, 0), (0, 1), (1, 1))
CUT = 256
WIDE_Y = 512 + CUT
WIDE_Z = 1024 - CUT


def call(body, outs, specs, *args, scratch=(), limit=2):
    return pl.pallas_call(
        body,
        out_shape=[jax.ShapeDtypeStruct(s, BF) for s in outs],
        in_specs=specs,
        out_specs=[VMEM] * len(outs),
        scratch_shapes=list(scratch),
        compiler_params=pltpu.CompilerParams(vmem_limit_bytes=limit * MIB),
    )(*args)


def copy_all(moves, sems):
    copies = [pltpu.make_async_copy(src, dst, sems.at[i]) for i, (src, dst) in enumerate(moves)]
    for copy in copies:
        copy.start()
    return copies


def transpose_halves(m_ref, mine_ref, other_ref):
    c = lax.axis_index("c")
    for k in range(2):
        for part in range(2):
            lanes = slice(part * 128, (part + 1) * 128)
            mine_ref[k, :, lanes] = m_ref[k, part, :, pl.ds(pl.multiple_of(c * 128, 128), 128)].T
            other_ref[k, :, lanes] = m_ref[k, part, :, pl.ds(pl.multiple_of((1 - c) * 128, 128), 128)].T


def join_halves(mine_ref, got_ref, out_ref):
    out_ref[:, :, :256] = mine_ref[...]
    out_ref[:, :, 256:] = got_ref[...]


def join(a_ref, b_ref, out_ref, sems):
    for copy in copy_all([(a_ref, out_ref.at[0]), (b_ref, out_ref.at[1])], sems):
        copy.wait()


def ring_masks(flip=0):
    c = lax.axis_index("c")
    c = 1 - c if flip else c
    return (0, 1 + 2 * c, 3 - 2 * c, 2)


def pair_row(list_ref, pair):
    row = 0
    for r in range(1, 3):
        row = jnp.where((list_ref[0, r] == pair[0]) & (list_ref[1, r] == pair[1]), r, row)
    return row


def weight_rows(list_ref, q_ref, own_ref, mate_ref, out_ref, held, sems):
    zl, y, c = lax.axis_index("zl"), lax.axis_index("y"), lax.axis_index("c")
    moves = []
    for slot in range(2):
        q = q_ref[pair_row(list_ref, PAIRS[slot])]
        for o, ref in enumerate((own_ref, mate_ref)):
            moves.append((ref.at[q], held.at[slot, o]))
    copies = copy_all(moves, sems)
    for slot in range(2):
        for o in range(2):
            copies[slot * 2 + o].wait()
            for b in range(2):
                for s, mask in enumerate(ring_masks(b)):
                    block = (zl ^ b) * 4 + (y ^ mask)
                    lanes = pl.ds(pl.multiple_of(block * 256 + c * 128, 128), 128)
                    re, im = held[slot, o, 0, :, lanes], held[slot, o, 1, :, lanes]
                    row, col = o * 256, (b * 4 + s) * 256
                    out_ref[slot, row : row + 128, col : col + 128] = re
                    out_ref[slot, row : row + 128, col + 128 : col + 256] = -im
                    out_ref[slot, row + 128 : row + 256, col : col + 128] = im
                    out_ref[slot, row + 128 : row + 256, col + 128 : col + 256] = re


def screen(w_ref, *refs):
    pieces, outs, (acc, held, sems) = refs[:4], refs[4:7], refs[7:]
    copies = copy_all([(ref, held.at[i]) for i, ref in enumerate(pieces)], sems)
    for i in range(2):
        copies[2 * i].wait()
        copies[2 * i + 1].wait()
        cols = slice(i * 1024, (i + 1) * 1024)
        for p, (k, kp) in enumerate(PAIRS):
            rhs = held[2 * i : 2 * i + 2, :, kp].reshape(1024, 256)
            term = jnp.dot(w_ref[kp - k, :, cols], rhs, preferred_element_type=F32)
            if i == 0:
                acc[p] = term
            else:
                acc[p] += term
    for p, ref in enumerate(outs):
        ref[...] = acc[p].reshape(2, 2, 128, 256).astype(BF)


def right_side(mine_ref, got_ref):
    blocks = []
    for o in range(2):
        re = (mine_ref[o, 0].astype(F32) + got_ref[1 - o, 0].astype(F32)).astype(BF)
        im = (mine_ref[o, 1].astype(F32) + got_ref[1 - o, 1].astype(F32)).astype(BF)
        blocks += [jnp.concatenate((re, im), 1), jnp.concatenate((im, -re), 1)]
    return jnp.concatenate(blocks, 0)


def rows_for(b, s, k, pieces):
    x, zh, zl, y, c = (lax.axis_index(a) for a in ("x", "zh", "zl", "y", "c"))
    j = (zl ^ b) * 4 + lax.rem(y + s, 4)
    mask = (j // 2) ^ x
    same = lax.rem(j, 2) == zh
    first = jnp.where(same, 1 + 2 * c, 3 - 2 * c)
    near = (mask == 0) | (mask == first)
    unit = jnp.where((mask == 0) | (mask == 4 - first), 0, 1)
    values = [ref[unit, k] for ref in pieces]
    own = jnp.where(near, values[0], values[1])
    far = jnp.where(near, values[2], values[3])
    return jnp.where(same, own, far)


def contract_y(factor, m0_ref, g0_ref, m1_ref, g1_ref, r0, r1, r2, r3, k_ref, s1_ref, s2_ref, s3_ref, rest_ref):
    rhs = [right_side(m0_ref, g0_ref), right_side(m1_ref, g1_ref)]
    for b in range(2):
        for s, ref in enumerate((k_ref, s1_ref, s2_ref, s3_ref)):
            rows = rows_for(b, s, 0, (r0, r1, r2, r3))
            for p in range(2):
                part = jnp.dot(rows, rhs[p], preferred_element_type=F32)
                part = (part * factor).astype(BF)
                if p == 0:
                    ref[b, :, :512] = part
                else:
                    ref[b, :, 512:] = part[:, :CUT]
                    rest_ref[b, s] = part[:, CUT:]


def contract_z(factor, mine_ref, got_ref, r0, r1, r2, r3, rest_ref, k_ref, s_ref):
    rhs = right_side(mine_ref, got_ref)
    for b, ref in enumerate((k_ref, s_ref)):
        for s in range(4):
            part = jnp.dot(rows_for(b, s, 1, (r0, r1, r2, r3)), rhs, preferred_element_type=F32)
            ref[s, :, :512] = (part * factor).astype(BF)
            ref[s, :, 512:] = rest_ref[b, s]


def add_z(keep_ref, got_ref, *outs):
    for s, ref in enumerate(outs):
        ref[...] = (keep_ref[s].astype(F32) + got_ref[s].astype(F32)).astype(BF)


def add_y(keep_ref, g1_ref, g2_ref, g3_ref, after_ref, out_ref, send_ref):
    for b, ref in enumerate((out_ref, send_ref)):
        near = keep_ref[b].astype(F32) + g1_ref[b].astype(F32)
        ref[...] = (near + (g2_ref[b].astype(F32) + g3_ref[b].astype(F32))).astype(BF)


def finish(list_ref, z0_ref, z1_ref, z2_ref, z3_ref, y0_ref, y1_ref, out_ref):
    z = z0_ref[...].astype(F32) + z1_ref[...].astype(F32) + (z2_ref[...].astype(F32) + z3_ref[...].astype(F32))
    y = y0_ref[...].astype(F32) + y1_ref[...].astype(F32)
    sums = (y[:, :512], jnp.concatenate((y[:, 512:], z[:, 512:]), 1), z[:, :512])
    for pair, value in zip(PAIRS, sums):
        out_ref[pair_row(list_ref, pair)] = value.astype(BF)


def shift(x, axis, size, step):
    return lax.ppermute(x, axis, [(i, (i + step) % size) for i in range(size)])


def ring_swap(x, axis, second):
    pairs = [(i * 2 + c, (i ^ (3 if c ^ second else 1)) * 2 + c) for i in range(4) for c in range(2)]
    return lax.ppermute(x, (axis, "c"), pairs)


def double(x, got):
    return call(join, [(2,) + x.shape], [ANY] * 2, x, got, scratch=[pltpu.SemaphoreType.DMA((2,))])[0]


def tie(*xs):
    return lax.optimization_barrier(xs)


def per_device(matrix_elements, screening, pair_list, pair_q):
    factor = 1.0 / math.sqrt(2.0 * screening.shape[3])
    m, pairs = matrix_elements, pair_list.T
    mine, other = call(transpose_halves, [(2, 128, 256)] * 2, [VMEM], m)
    (rows,) = call(join_halves, [(2, 128, 512)], [VMEM] * 2, mine, shift(other, "c", 2, 1))
    mate_weights = shift(screening, "c", 2, 1)
    m_far = shift(m, "zl", 2, 1)
    m_got = ring_swap(m, "y", 0)
    rows_far = shift(rows, "zh", 2, 1)
    rows_got = ring_swap(rows, "x", 0)
    m_near = double(m, m_got)
    m_next = ring_swap(m_near, "y", 1)
    rows_near = double(rows, rows_got)
    rows_next = ring_swap(rows_near, "x", 1)
    m_far_got = ring_swap(m_far, "y", 1)
    m_far_got, rows_far = tie(m_far_got, rows_far)
    rows_far_got = ring_swap(rows_far, "x", 1)
    m_far_near = double(m_far, m_far_got)
    m_far_next = ring_swap(m_far_near, "y", 0)
    rows_far_near = double(rows_far, rows_far_got)
    rows_far_next = ring_swap(rows_far_near, "x", 0)
    (weights,) = call(
        weight_rows,
        [(2, 512, 2048)],
        [SMEM] * 2 + [ANY] * 2,
        pairs,
        pair_q,
        screening,
        mate_weights,
        limit=8,
        scratch=[pltpu.VMEM((2, 2, 2, 128, 2048), BF), pltpu.SemaphoreType.DMA((4,))],
    )
    weights, rows_next = tie(weights, rows_next)
    parts = call(
        screen,
        [(2, 2, 128, 256)] * 3,
        [VMEM] + [ANY] * 4,
        weights,
        m_near,
        m_next,
        m_far_near,
        m_far_next,
        limit=8,
        scratch=[pltpu.VMEM((3, 512, 256), F32), pltpu.VMEM((4, 2, 2, 2, 128, 256), BF), pltpu.SemaphoreType.DMA((4,))],
    )
    sides = [(part, shift(part, "c", 2, 1)) for part in parts]
    left = [rows_near, rows_next, rows_far_near, rows_far_next]
    y_keep, y1, y2, y3, rest = call(
        functools.partial(contract_y, factor),
        [(2, 128, WIDE_Y)] * 4 + [(2, 4, 128, 512 - CUT)],
        [VMEM] * 8,
        *sides[0],
        *sides[1],
        *left,
        limit=8,
    )
    z_keep, z_send = call(
        functools.partial(contract_z, factor), [(4, 128, WIDE_Z)] * 2, [VMEM] * 7, *sides[2], *left, rest, limit=8
    )
    z_got = shift(z_send, "zl", 2, 1)
    y_got = [shift(y1, "y", 4, 1), shift(y3, "y", 4, -1), shift(y2, "y", 4, 2)]
    z_sums = call(add_z, [(128, WIDE_Z)] * 4, [VMEM] * 2, z_keep, z_got)
    y_keep, y_send = call(add_y, [(128, WIDE_Y)] * 2, [VMEM] * 4 + [ANY], y_keep, *y_got, z_sums[0])
    z_last = [shift(z_sums[2], "y", 4, 2), shift(z_sums[1], "y", 4, 1), shift(z_sums[3], "y", 4, -1)]
    y_last = shift(y_send, "zl", 2, 1)
    (out,) = call(finish, [(3, 128, 512)], [SMEM] + [VMEM] * 6, pairs, z_sums[0], *z_last, y_keep, y_last)
    return out.reshape(3, 128, 2, 256)


def solution(mesh):
    split = Mesh(mesh.devices.reshape(4, 2, 2, 4, 2), ("x", "zh", "zl", "y", "c"))
    ga = ("zl", "y", "c")
    return jax.shard_map(
        per_device,
        mesh=split,
        in_specs=(P(None, None, ga, ("x", "zh")), P(None, None, ga, None), P(), P()),
        out_specs=P(None, ga, None, ("x", "zh")),
        check_vma=False,
    )
```
